32 devices in a mesh: win: 2 (over x), sta: 16 (over z, y, core).
Axes of the slice: x: 2, y: 2, z: 4, core: 2. Of those that a mesh axis runs over, the one named last changes fastest.
Arguments:
- records: bfloat16 [1024, 16384], P('win', 'sta'), parts along dimension 0, may hold values from -600 to 600
- filter_taps: bfloat16 [129], replicated, may hold values from -0.5 to 0.5
- ref_owner: int32 [4], P('win'), parts along dimension 0, may hold values from 0 to 15
- reference_station_order: int32 [4, 32], P('win'), parts along dimension 0, may hold values from 0 to 31, each once within a row
- pair_valid: int32 [4, 32, 512], P('win', None, 'sta'), parts along dimension 0, may hold values 0 or 1
Outputs:
- correlations: float32 [4, 32, 512, 256], P('win', None, 'sta'), parts along dimension 0
The draws below stay inside these ranges and needn't reach their ends.
There are 2 independent parts, one for each index of `win`. The reference program is written for one: setup_inputs(seed, part) draws one part's arguments, and reference() takes and returns one part's arrays. A program takes and returns all parts, laid end to end along the dimension named above; an argument that names none is the same for every part. Nothing has to cross between parts.
Inputs may be any that keep to these rules, and one draw needn't show every extreme that they name: Each row of reference_station_order is a permutation of 0 .. 31.
All inputs are finite; a program needn't handle non-finite values. No bound on the sum of `pair_valid` on one device may be relied on, other than what follows from the above.
Results may differ from the reference program's by a relative error of at most 0.0073.
Values may be sent and summed in bfloat16 or wider, within the bound.
A program may use at most 128 MiB of HBM per device.

```python
import math
import jax
import jax.numpy as jnp
from jax import lax

STA_DEV = 32
STATIONS = 512
NFFT = 1024
TRACE_SAMPLES = 16384
TAPS = 129
LAGS = 256
STEPS = 2
N_STA = 16


def draw_records(key, part):
    key_noise = jax.random.fold_in(key, 11)
    key_station = jax.random.fold_in(key, 12)
    pulse_seed_state = jax.random.fold_in(key, 13)
    samples = jnp.clip(jax.random.normal(key_noise, (STATIONS, TRACE_SAMPLES), jnp.float32), -6.0, 6.0)
    station_scale = jnp.exp(jax.random.uniform(key_station, (STATIONS, 1), jnp.float32, 0.0, math.log(10.0)))
    transient_pulses = jnp.exp(jax.random.uniform(pulse_seed_state, (1, TRACE_SAMPLES // 32), jnp.float32, 0.0, math.log(10.0)))
    duration_factor = jnp.repeat(transient_pulses, 32, axis=1)
    return (samples * station_scale * duration_factor).astype(jnp.bfloat16)


def with_ends(values, own_key, least, largest):
    longest = values.shape.index(max(values.shape))
    spots = []
    for shift in (0, 1):
        where = [jax.random.randint(jax.random.fold_in(own_key, axis), (), 0, length) for axis, length in enumerate(values.shape)]
        where[longest] = (where[longest] + shift) % values.shape[longest]
        spots.append(tuple(where))
    return values.at[spots[0]].set(least).at[spots[1]].set(largest)


def centred(key, extent, scale, limit, held_as=jnp.bfloat16):
    result = scale * jax.random.normal(key, extent, jnp.float32)
    return jnp.clip(result, min=-limit, max=limit).astype(held_as)


def setup_inputs(seed: int = 0, part: int = 0) -> dict:
    key_list = jax.random.split(jax.random.key(seed), 6)
    part_splits = jax.random.split(jax.random.fold_in(key_list[5], part), 6)
    records = draw_records(jax.random.fold_in(jax.random.fold_in(key_list[5], part), 71), part)
    filter_taps = centred(key_list[1], (TAPS,), TAPS ** -0.5, 0.5)
    ref_owner = jax.random.randint(part_splits[2], (STEPS,), 0, N_STA).astype(jnp.int32)
    reference_station_order = jax.vmap(lambda own: jax.random.permutation(own, STA_DEV))(jax.random.split(part_splits[3], STEPS)).reshape((STEPS, STA_DEV)).astype(jnp.int32)
    pair_valid = with_ends((jax.random.randint(part_splits[4], (STEPS, STA_DEV, STATIONS), 0, 4) < 3).astype(jnp.int32), jax.random.fold_in(part_splits[4], 1), 0, 1)
    return {"records": records, "filter_taps": filter_taps, "ref_owner": ref_owner, "reference_station_order": reference_station_order, "pair_valid": pair_valid}


def forward_matrix(length):
    time_index = jnp.arange(length, dtype=jnp.int32)[:, None]
    bin_index = jnp.arange(length // 2, dtype=jnp.int32)[None, :]
    angles = (time_index * bin_index % length).astype(jnp.float32) * (2.0 * math.pi / length)
    return jnp.concatenate([jnp.cos(angles), -jnp.sin(angles)], axis=1).astype(jnp.bfloat16)

def inverse_transform_matrix(length, lag_count, segments):
    bin_index = jnp.arange(length // 2, dtype=jnp.int32)[:, None]
    shifts = jnp.arange(lag_count, dtype=jnp.int32)[None, :] - lag_count // 2
    angles = (bin_index * shifts % length).astype(jnp.float32) * (2.0 * math.pi / length)
    factor = 1.0 / math.sqrt(segments * (length // 2))
    return jnp.concatenate([factor * jnp.cos(angles), -factor * jnp.sin(angles)], axis=0).astype(jnp.bfloat16)

def flatten_amplitudes(fourier_coefficients):
    bin_count = fourier_coefficients.shape[-1] // 2
    real_part = fourier_coefficients[..., :bin_count]
    imag_part = fourier_coefficients[..., bin_count:]
    energy = real_part * real_part + imag_part * imag_part
    water_level = lax.optimization_barrier(jnp.mean(energy, axis=-1, keepdims=True))
    factor = lax.rsqrt(energy + water_level + 1e-06)
    return jnp.concatenate([real_part * factor, imag_part * factor], axis=-1).astype(jnp.bfloat16)

def correlate(chosen, resident, inverse):
    bin_count = chosen.shape[-1] // 2
    ref_stack = jnp.stack([chosen[..., :bin_count], chosen[..., bin_count:]], axis=2).astype(jnp.float32)
    direct = jnp.stack([resident[..., :bin_count], resident[..., bin_count:]], axis=2).astype(jnp.float32)
    rotated = jnp.stack([-resident[..., bin_count:], resident[..., :bin_count]], axis=2).astype(jnp.float32)
    real_sum = jnp.einsum('rgcf,sgcf->rsf', ref_stack, direct, precision=lax.Precision.HIGHEST)
    imag_sum = jnp.einsum('rgcf,sgcf->rsf', ref_stack, rotated, precision=lax.Precision.HIGHEST)
    cross = jnp.concatenate([real_sum, imag_sum], axis=-1).astype(jnp.bfloat16)
    ref_count = chosen.shape[0]
    own_count = resident.shape[0]
    lagged = jnp.dot(cross.reshape(ref_count * own_count, 2 * bin_count).astype(jnp.float32), inverse.astype(jnp.float32), precision=lax.Precision.HIGHEST)
    return lagged.reshape(ref_count, own_count, inverse.shape[1])

def reference(records, filter_taps, ref_owner, reference_station_order, pair_valid):
    stations, length = records.shape
    margin = (filter_taps.shape[0] - 1) // 2
    signal = records.astype(jnp.float32)[:, None, :]
    kernel = filter_taps.astype(jnp.float32)[None, None, :]
    filtered_signal = lax.conv_general_dilated(signal, kernel, (1,), [(margin, margin)], precision=lax.Precision.HIGHEST)[:, 0, :].astype(jnp.bfloat16)
    segments = length // NFFT
    fourier_coefficients = jnp.dot(filtered_signal.reshape(stations * segments, NFFT).astype(jnp.float32), forward_matrix(NFFT).astype(jnp.float32), precision=lax.Precision.HIGHEST)
    whitened = flatten_amplitudes(fourier_coefficients.reshape(stations, segments, NFFT))
    inverse = inverse_transform_matrix(NFFT, LAGS, segments)
    resident_blocks = whitened.reshape(N_STA, STA_DEV, segments, NFFT)
    results = []
    for running_total in range(STEPS):
        start_row = (ref_owner[running_total] * STA_DEV).astype(jnp.int32)
        owned = lax.dynamic_slice_in_dim(whitened, start_row, STA_DEV, 0)
        chosen = jnp.take(owned, reference_station_order[running_total].astype(jnp.int32), axis=0)

        def per_block(resident):
            return correlate(chosen, resident, inverse)
        accumulated_sum = lax.map(per_block, resident_blocks)
        merged = jnp.transpose(accumulated_sum, (1, 0, 2, 3)).reshape(STA_DEV, stations, LAGS)
        results.append(merged * pair_valid[running_total].astype(jnp.float32)[:, :, None])
    return jnp.stack(results)
```

```python
import math

import jax
import jax.numpy as jnp
from jax import lax
from jax.sharding import PartitionSpec as P

NFFT = 1024
LAGS = 256
STEPS = 2


def forward_matrix(length):
    time_index = jnp.arange(length, dtype=jnp.int32)[:, None]
    bin_index = jnp.arange(length // 2, dtype=jnp.int32)[None, :]
    angles = (time_index * bin_index % length).astype(jnp.float32) * (2.0 * math.pi / length)
    return jnp.concatenate([jnp.cos(angles), -jnp.sin(angles)], axis=1).astype(jnp.bfloat16)


def inverse_transform_matrix(length, lag_count, segments):
    bin_index = jnp.arange(length // 2, dtype=jnp.int32)[:, None]
    shifts = jnp.arange(lag_count, dtype=jnp.int32)[None, :] - lag_count // 2
    angles = (bin_index * shifts % length).astype(jnp.float32) * (2.0 * math.pi / length)
    factor = 1.0 / math.sqrt(segments * (length // 2))
    return jnp.concatenate([factor * jnp.cos(angles), -factor * jnp.sin(angles)], axis=0).astype(
        jnp.bfloat16
    )


def flatten_amplitudes(fourier_coefficients):
    bin_count = fourier_coefficients.shape[-1] // 2
    real_part = fourier_coefficients[..., :bin_count]
    imag_part = fourier_coefficients[..., bin_count:]
    energy = real_part * real_part + imag_part * imag_part
    water_level = jnp.mean(energy, axis=-1, keepdims=True)
    factor = lax.rsqrt(energy + water_level + 1e-06)
    return jnp.concatenate([real_part * factor, imag_part * factor], axis=-1).astype(jnp.bfloat16)


def spectra_of(station_rows, filter_taps):
    row_count, length = station_rows.shape
    tap_count = filter_taps.shape[0]
    margin = (tap_count - 1) // 2
    offsets = (
        jnp.arange(384, dtype=jnp.int32)[:, None]
        - jnp.arange(128, dtype=jnp.int32)[None, :]
        - 128
        + margin
    )
    match_flags = offsets[:, :, None] == jnp.arange(tap_count, dtype=jnp.int32)[None, None, :]
    banded = jnp.sum(
        jnp.where(match_flags, filter_taps.astype(jnp.float32)[None, None, :], 0.0), axis=2
    ).astype(jnp.bfloat16)
    padded = jnp.pad(station_rows, ((0, 0), (128, 128)))
    pieces = padded.reshape(row_count, length // 128 + 2, 128)
    windows = jnp.concatenate([pieces[:, :-2], pieces[:, 1:-1], pieces[:, 2:]], axis=2)
    filtered_signal = jnp.einsum(
        "nbu,uv->nbv", windows, banded, preferred_element_type=jnp.float32
    ).astype(jnp.bfloat16)
    segments = length // NFFT
    fourier_coefficients = jnp.dot(
        filtered_signal.reshape(row_count * segments, NFFT),
        forward_matrix(NFFT),
        preferred_element_type=jnp.float32,
    )
    return flatten_amplitudes(fourier_coefficients.reshape(row_count, segments, NFFT))


def correlate(chosen, resident, inverse):
    bin_count = chosen.shape[-1] // 2
    ref_stack = jnp.stack([chosen[..., :bin_count], chosen[..., bin_count:]], axis=2)
    direct = jnp.stack([resident[..., :bin_count], resident[..., bin_count:]], axis=2)
    rotated = jnp.stack([-resident[..., bin_count:], resident[..., :bin_count]], axis=2)
    real_sum = jnp.einsum("rgcf,sgcf->rsf", ref_stack, direct, preferred_element_type=jnp.float32)
    imag_sum = jnp.einsum("rgcf,sgcf->rsf", ref_stack, rotated, preferred_element_type=jnp.float32)
    cross = jnp.concatenate([real_sum, imag_sum], axis=-1).astype(jnp.bfloat16)
    ref_count = chosen.shape[0]
    own_count = resident.shape[0]
    lagged = jnp.dot(
        cross.reshape(ref_count * own_count, 2 * bin_count),
        inverse,
        preferred_element_type=jnp.float32,
    )
    return lagged.reshape(ref_count, own_count, inverse.shape[1])


def local(records, filter_taps, ref_owner, reference_station_order, pair_valid):
    device_count = lax.axis_size("sta")
    own_count = records.shape[0] // device_count
    order = ref_owner[:, None] * own_count + reference_station_order
    ref_rows = jnp.take(records, order.reshape(-1), axis=0)
    ref_rows = lax.all_gather(ref_rows, "sta", axis=1, tiled=True)
    station_rows = lax.all_to_all(records, "sta", split_axis=0, concat_axis=1, tiled=True)
    whitened = spectra_of(jnp.concatenate([station_rows, ref_rows], axis=0), filter_taps)
    inverse = inverse_transform_matrix(NFFT, LAGS, whitened.shape[1])
    lagged = correlate(whitened[own_count:], whitened[:own_count], inverse)
    lagged = lagged.reshape(STEPS, -1, own_count, LAGS)
    return lagged * pair_valid.astype(jnp.float32)[..., None]


def solution(mesh):
    placed = (P("win", "sta"), P(), P("win"), P("win", None), P("win", None, "sta"))
    return jax.shard_map(
        local, mesh=mesh, in_specs=placed, out_specs=P("win", None, "sta", None), check_vma=False
    )
```

```python
import math

import jax
import jax.numpy as jnp
import ml_dtypes
import numpy as np
from jax import lax
from jax.experimental import pallas as pl
from jax.experimental.pallas import tpu as pltpu
from jax.sharding import PartitionSpec as P

NFFT = 1024
LAGS = 256
BINS = NFFT // 2
LANES = 128
MIB = 1 << 20


def forward_padded():
    product = np.arange(BINS)[:, None] * np.arange(NFFT)[None, :] % NFFT
    angles = product * (2.0 * math.pi / NFFT)
    rows = np.concatenate([np.cos(angles), -np.sin(angles)], axis=0)
    return np.pad(rows, ((0, 0), (256, 256))).astype(np.float32).astype(ml_dtypes.bfloat16)


def inverse_rows(segments):
    product = np.arange(BINS)[None, :] * (np.arange(LAGS)[:, None] - LAGS // 2) % NFFT
    angles = product * (2.0 * math.pi / NFFT)
    factor = 1.0 / math.sqrt(segments * BINS)
    rows = np.concatenate([factor * np.cos(angles), -factor * np.sin(angles)], axis=1)
    return rows.astype(np.float32).astype(ml_dtypes.bfloat16)


def band(filter_taps):
    tap_count = filter_taps.shape[0]
    margin = (tap_count - 1) // 2
    offsets = (
        jnp.arange(LANES, dtype=jnp.int32)[None, :]
        - jnp.arange(3 * LANES, dtype=jnp.int32)[:, None]
        + LANES
        + margin
    )
    match = offsets[:, :, None] == jnp.arange(tap_count, dtype=jnp.int32)[None, None, :]
    return jnp.sum(
        jnp.where(match, filter_taps.astype(jnp.float32)[None, None, :], 0.0), axis=2
    ).astype(jnp.bfloat16)


def fold_kernel(forward_ref, band_ref, fold_ref):
    for j in range(fold_ref.shape[1] // LANES):
        fold_ref[:, j * LANES : (j + 1) * LANES] = jnp.dot(
            forward_ref[:, j * LANES : (j + 3) * LANES],
            band_ref[...],
            preferred_element_type=jnp.float32,
        ).astype(fold_ref.dtype)


def folded(filter_taps):
    return pl.pallas_call(
        fold_kernel,
        out_shape=jax.ShapeDtypeStruct((NFFT, NFFT + 2 * LANES), jnp.bfloat16),
        compiler_params=pltpu.CompilerParams(vmem_limit_bytes=32 * MIB),
    )(jnp.asarray(forward_padded()), band(filter_taps))


def main_kernel(fold_ref, own_ref, refs_ref, inv_ref, valid_ref, out_ref, x, y, w, o, v, z):
    segments, own, _ = own_ref.shape
    refs = refs_ref.shape[1]
    pairs = segments // 2
    depth = 2 * segments
    dot = lambda a, b, ca, cb: lax.dot_general(
        a, b, (((ca,), (cb,)), ((), ())), preferred_element_type=jnp.float32
    )

    for g in range(segments):
        base = (g % 2) * LANES
        places = ((0, own, own_ref), (own, own, own_ref), (2 * own, refs, refs_ref))
        for start, count, source in places:
            rows = slice(base + start, base + start + count)
            edge = jnp.zeros((count, LANES), x.dtype)
            x[g // 2, rows, LANES : LANES + NFFT] = source[g]
            x[g // 2, rows, :LANES] = source[g - 1, :, NFFT - LANES :] if g else edge
            x[g // 2, rows, LANES + NFFT :] = (
                source[g + 1, :, :LANES] if g + 1 < segments else edge
            )

    chunk = 64

    def transform(p, carry):
        y[...] = dot(fold_ref[...], x[p], 1, 1)
        lane = lax.broadcasted_iota(jnp.int32, (chunk, LANES), 1)
        turned = (lane >= own) & (lane < 2 * own)
        for h in range(2):
            columns = slice(h * LANES, (h + 1) * LANES)
            total = jnp.zeros((chunk, LANES), jnp.float32)
            for c in range(BINS // chunk):
                re = y[c * chunk : (c + 1) * chunk, columns]
                im = y[BINS + c * chunk : BINS + (c + 1) * chunk, columns]
                total += re * re + im * im
            water = jnp.sum(total, axis=0, keepdims=True) * (1.0 / BINS)
            for c in range(BINS // chunk):
                re = y[c * chunk : (c + 1) * chunk, columns]
                im = y[BINS + c * chunk : BINS + (c + 1) * chunk, columns]
                factor = lax.rsqrt(re * re + im * im + water + 1e-06)
                a, b = re * factor, im * factor
                at = c * chunk * depth + 2 * p + h
                w[pl.ds(at, chunk, stride=depth), :] = jnp.where(turned, -b, a)
                w[pl.ds(at + segments, chunk, stride=depth), :] = jnp.where(turned, a, b)
        return carry

    lax.fori_loop(0, pairs, transform, 0)

    group = LANES // depth
    both = 2 * own

    def cross(q, carry):
        t = w[pl.ds(pl.multiple_of(q * LANES, LANES), LANES), :]
        lane = lax.broadcasted_iota(jnp.int32, (LANES, LANES), 1)
        row = lax.broadcasted_iota(jnp.int32, (LANES, LANES), 0)
        left = t.T[:both].astype(jnp.bfloat16)
        twice = jnp.where(lane < refs, pltpu.roll(t, LANES - both, 1), t)
        right = jnp.concatenate(
            [
                jnp.where((row >= j * depth) & (row < (j + 1) * depth), twice, 0.0)
                for j in range(group)
            ],
            axis=1,
        ).astype(jnp.bfloat16)
        product = dot(left, right, 1, 0)
        for j in range(group):
            at = pl.multiple_of((q * group + j) * both, both)
            o[pl.ds(at, both), :] = product[:, j * LANES : (j + 1) * LANES]
        return carry

    lax.fori_loop(0, BINS // group, cross, 0, unroll=2)

    def lags(n, carry):
        lane = lax.broadcasted_iota(jnp.int32, (BINS, LANES), 1)
        for j in range(2):
            for c in range(2):
                at = c * own + 4 * n + 2 * j
                a = o[pl.ds(at, BINS, stride=both), :]
                b = o[pl.ds(at + 1, BINS, stride=both), :]
                v[c * BINS : (c + 1) * BINS, j * LANES : (j + 1) * LANES] = jnp.where(
                    lane < refs, a, b
                ).astype(v.dtype)
        lagged = dot(inv_ref[...], v[...], 1, 0) * valid_ref[n]
        turned = lagged.T
        for i in range(4):
            for h in range(LAGS // LANES):
                z[h, pl.ds(4 * n + i, refs, stride=own), :] = turned[
                    i * refs : (i + 1) * refs, h * LANES : (h + 1) * LANES
                ]
        return carry

    lax.fori_loop(0, own // 4, lags, 0)
    for h in range(LAGS // LANES):
        out_ref[:, h * LANES : (h + 1) * LANES] = z[h]


def compute(fold, own_rows, ref_rows, pair_valid):
    segments, own, _ = own_rows.shape
    refs = ref_rows.shape[1]
    valid = pair_valid.reshape(refs, own).astype(jnp.float32).T.reshape(own // 4, 1, 4 * refs)
    f32, bf16 = jnp.float32, jnp.bfloat16
    return pl.pallas_call(
        main_kernel,
        out_shape=jax.ShapeDtypeStruct((refs * own, LAGS), f32),
        scratch_shapes=[
            pltpu.VMEM((segments // 2, 2 * LANES, NFFT + 2 * LANES), bf16),
            pltpu.VMEM((NFFT, 2 * LANES), f32),
            pltpu.VMEM((BINS * 2 * segments, LANES), f32),
            pltpu.VMEM((BINS * 2 * own, LANES), f32),
            pltpu.VMEM((NFFT, 2 * LANES), bf16),
            pltpu.VMEM((LAGS // LANES, refs * own, LANES), f32),
        ],
        compiler_params=pltpu.CompilerParams(vmem_limit_bytes=52 * MIB),
    )(fold, own_rows, ref_rows, jnp.asarray(inverse_rows(segments)), valid)


def by_segment(blocks):
    devices, stations, samples = blocks.shape
    if samples == NFFT:
        return blocks
    return (
        blocks.transpose(1, 0, 2)
        .reshape(stations, devices * samples // NFFT, NFFT)
        .transpose(1, 0, 2)
    )


def local(records, filter_taps, ref_owner, reference_station_order, pair_valid):
    device_count = lax.axis_size("sta")
    stations, samples = records.shape
    own = stations // device_count
    order = ref_owner[:, None] * own + reference_station_order
    ref_rows = jnp.take(records, order.reshape(-1), axis=0)
    ref_rows = lax.all_gather(ref_rows, "sta", axis=0, tiled=False)
    own_rows = lax.all_to_all(
        records.reshape(device_count, own, samples), "sta", split_axis=0, concat_axis=0, tiled=True
    )
    out = compute(folded(filter_taps), by_segment(own_rows), by_segment(ref_rows), pair_valid)
    return out.reshape(pair_valid.shape + (LAGS,))


def solution(mesh):
    placed = (P("win", "sta"), P(), P("win"), P("win", None), P("win", None, "sta"))
    return jax.shard_map(
        local, mesh=mesh, in_specs=placed, out_specs=P("win", None, "sta", None), check_vma=False
    )
```

```python
import math

import jax
import jax.numpy as jnp
import ml_dtypes
import numpy as np
from jax import lax
from jax.experimental import pallas as pl
from jax.experimental.pallas import tpu as pltpu
from jax.sharding import PartitionSpec as P

NFFT = 1024
LAGS = 256
BINS = NFFT // 2
LANES = 128
SKEW = 8
MIB = 1 << 20


def forward_padded():
    product = np.arange(BINS)[:, None] * np.arange(NFFT)[None, :] % NFFT
    angles = product * (2.0 * math.pi / NFFT)
    rows = np.concatenate([np.cos(angles), -np.sin(angles)], axis=0)
    return np.pad(rows, ((0, 0), (256, 256))).astype(np.float32).astype(ml_dtypes.bfloat16)


def inverse_rows(segments):
    product = np.arange(BINS)[None, :] * (np.arange(LAGS)[:, None] - LAGS // 2) % NFFT
    angles = product * (2.0 * math.pi / NFFT)
    factor = 1.0 / math.sqrt(segments * BINS)
    rows = np.concatenate([factor * np.cos(angles), -factor * np.sin(angles)], axis=1)
    return rows.astype(np.float32).astype(ml_dtypes.bfloat16)


def band(filter_taps):
    tap_count = filter_taps.shape[0]
    margin = (tap_count - 1) // 2
    offsets = (
        jnp.arange(LANES, dtype=jnp.int32)[None, :]
        - jnp.arange(3 * LANES, dtype=jnp.int32)[:, None]
        + LANES
        + margin
    )
    match = offsets[:, :, None] == jnp.arange(tap_count, dtype=jnp.int32)[None, None, :]
    return jnp.sum(
        jnp.where(match, filter_taps.astype(jnp.float32)[None, None, :], 0.0), axis=2
    ).astype(jnp.bfloat16)


def fold_kernel(forward_ref, band_ref, fold_ref):
    for j in range(fold_ref.shape[1] // LANES):
        fold_ref[:, j * LANES : (j + 1) * LANES] = jnp.dot(
            forward_ref[:, j * LANES : (j + 3) * LANES],
            band_ref[...],
            preferred_element_type=jnp.float32,
        ).astype(fold_ref.dtype)


def folded(filter_taps):
    return pl.pallas_call(
        fold_kernel,
        out_shape=jax.ShapeDtypeStruct((NFFT, NFFT + 2 * LANES), jnp.bfloat16),
        compiler_params=pltpu.CompilerParams(vmem_limit_bytes=32 * MIB),
    )(jnp.asarray(forward_padded()), band(filter_taps))


def main_kernel(fold_ref, own_ref, refs_ref, inv_ref, valid_ref, out_ref, x, y, w, o, v, z):
    segments, own, _ = own_ref.shape
    refs = refs_ref.shape[1]
    pairs = segments // 2
    depth = 2 * segments
    dot = lambda a, b, ca, cb: lax.dot_general(
        a, b, (((ca,), (cb,)), ((), ())), preferred_element_type=jnp.float32
    )

    for g in range(segments):
        base = (g % 2) * LANES
        places = ((0, own, own_ref), (own, own, own_ref), (2 * own, refs, refs_ref))
        for start, count, source in places:
            rows = slice(base + start, base + start + count)
            edge = jnp.zeros((count, LANES), x.dtype)
            x[g // 2, rows, LANES : LANES + NFFT] = source[g]
            x[g // 2, rows, :LANES] = source[g - 1, :, NFFT - LANES :] if g else edge
            x[g // 2, rows, LANES + NFFT :] = (
                source[g + 1, :, :LANES] if g + 1 < segments else edge
            )

    chunk = 64

    def transform(p, carry):
        y[...] = dot(fold_ref[...], x[p], 1, 1)
        lane = lax.broadcasted_iota(jnp.int32, (chunk, LANES), 1)
        turned = (lane >= own) & (lane < 2 * own)
        for h in range(2):
            columns = slice(h * LANES, (h + 1) * LANES)
            total = jnp.zeros((chunk, LANES), jnp.float32)
            for c in range(BINS // chunk):
                re = y[c * chunk : (c + 1) * chunk, columns]
                im = y[BINS + c * chunk : BINS + (c + 1) * chunk, columns]
                total += re * re + im * im
            water = jnp.sum(total, axis=0, keepdims=True) * (1.0 / BINS)
            for c in range(BINS // chunk):
                re = y[c * chunk : (c + 1) * chunk, columns]
                im = y[BINS + c * chunk : BINS + (c + 1) * chunk, columns]
                factor = lax.rsqrt(re * re + im * im + water + 1e-06)
                a, b = re * factor, im * factor
                at = c * chunk * (depth + SKEW) + 2 * p + h
                w[pl.ds(at, chunk, stride=depth + SKEW), :] = jnp.where(turned, -b, a)
                w[pl.ds(at + segments, chunk, stride=depth + SKEW), :] = jnp.where(turned, a, b)
        return carry

    lax.fori_loop(0, pairs, transform, 0)

    group = LANES // depth
    both = 2 * own

    def cross(q, carry):
        parts = [
            w[pl.ds(pl.multiple_of((q * group + j) * (depth + SKEW), 8), depth), :]
            for j in range(group)
        ]
        t = jnp.concatenate(parts, axis=0)
        lane = lax.broadcasted_iota(jnp.int32, (LANES, LANES), 1)
        row = lax.broadcasted_iota(jnp.int32, (LANES, LANES), 0)
        left = t.T[:both].astype(jnp.bfloat16)
        twice = jnp.where(lane < refs, pltpu.roll(t, LANES - both, 1), t)
        right = jnp.concatenate(
            [
                jnp.where((row >= j * depth) & (row < (j + 1) * depth), twice, 0.0)
                for j in range(group)
            ],
            axis=1,
        ).astype(jnp.bfloat16)
        product = dot(left, right, 1, 0)
        for j in range(group):
            at = pl.multiple_of((q * group + j) * (both + SKEW), 8)
            o[pl.ds(at, both), :] = product[:, j * LANES : (j + 1) * LANES]
        return carry

    lax.fori_loop(0, BINS // group, cross, 0, unroll=8)

    def lags(n, carry):
        lane = lax.broadcasted_iota(jnp.int32, (BINS, LANES), 1)
        for j in range(2):
            for c in range(2):
                at = c * own + 4 * n + 2 * j
                a = o[pl.ds(at, BINS, stride=both + SKEW), :]
                b = o[pl.ds(at + 1, BINS, stride=both + SKEW), :]
                v[c * BINS : (c + 1) * BINS, j * LANES : (j + 1) * LANES] = jnp.where(
                    lane < refs, a, b
                ).astype(v.dtype)
        lagged = dot(inv_ref[...], v[...], 1, 0) * valid_ref[n]
        turned = lagged.T
        for i in range(4):
            for h in range(LAGS // LANES):
                z[h, pl.ds(4 * n + i, refs, stride=own), :] = turned[
                    i * refs : (i + 1) * refs, h * LANES : (h + 1) * LANES
                ]
        return carry

    lax.fori_loop(0, own // 4, lags, 0, unroll=2)
    for h in range(LAGS // LANES):
        out_ref[:, h * LANES : (h + 1) * LANES] = z[h]


def compute(fold, own_rows, ref_rows, pair_valid):
    segments, own, _ = own_rows.shape
    refs = ref_rows.shape[1]
    valid = pair_valid.reshape(refs, own).astype(jnp.float32).T.reshape(own // 4, 1, 4 * refs)
    f32, bf16 = jnp.float32, jnp.bfloat16
    return pl.pallas_call(
        main_kernel,
        out_shape=jax.ShapeDtypeStruct((refs * own, LAGS), f32),
        scratch_shapes=[
            pltpu.VMEM((segments // 2, 2 * LANES, NFFT + 2 * LANES), bf16),
            pltpu.VMEM((NFFT, 2 * LANES), f32),
            pltpu.VMEM((BINS * (2 * segments + SKEW), LANES), f32),
            pltpu.VMEM((BINS * (2 * own + SKEW), LANES), f32),
            pltpu.VMEM((NFFT, 2 * LANES), bf16),
            pltpu.VMEM((LAGS // LANES, refs * own, LANES), f32),
        ],
        compiler_params=pltpu.CompilerParams(vmem_limit_bytes=52 * MIB),
    )(fold, own_rows, ref_rows, jnp.asarray(inverse_rows(segments)), valid)


def by_segment(blocks):
    devices, stations, samples = blocks.shape
    if samples == NFFT:
        return blocks
    return (
        blocks.transpose(1, 0, 2)
        .reshape(stations, devices * samples // NFFT, NFFT)
        .transpose(1, 0, 2)
    )


def local(records, filter_taps, ref_owner, reference_station_order, pair_valid):
    device_count = lax.axis_size("sta")
    stations, samples = records.shape
    own = stations // device_count
    order = ref_owner[:, None] * own + reference_station_order
    ref_rows = jnp.take(records, order.reshape(-1), axis=0)
    ref_rows = lax.all_gather(ref_rows, "sta", axis=0, tiled=False)
    own_rows = lax.all_to_all(
        records.reshape(device_count, own, samples), "sta", split_axis=0, concat_axis=0, tiled=True
    )
    out = compute(folded(filter_taps), by_segment(own_rows), by_segment(ref_rows), pair_valid)
    return out.reshape(pair_valid.shape + (LAGS,))


def solution(mesh):
    placed = (P("win", "sta"), P(), P("win"), P("win", None), P("win", None, "sta"))
    return jax.shard_map(
        local, mesh=mesh, in_specs=placed, out_specs=P("win", None, "sta", None), check_vma=False
    )
```

```python
import math

import jax
import jax.numpy as jnp
import ml_dtypes
import numpy as np
from jax import lax
from jax.experimental import pallas as pl
from jax.experimental.pallas import tpu as pltpu
from jax.sharding import PartitionSpec as P

NFFT = 1024
LAGS = 256
BINS = NFFT // 2
LANES = 128
SKEW = 8
MIB = 1 << 20


def forward_padded():
    product = np.arange(BINS)[:, None] * np.arange(NFFT)[None, :] % NFFT
    angles = product * (2.0 * math.pi / NFFT)
    rows = np.concatenate([np.cos(angles), -np.sin(angles)], axis=0)
    return np.pad(rows, ((0, 0), (256, 256))).astype(np.float32).astype(ml_dtypes.bfloat16)


def inverse_rows(segments):
    product = np.arange(BINS)[None, :] * (np.arange(LAGS)[:, None] - LAGS // 2) % NFFT
    angles = product * (2.0 * math.pi / NFFT)
    factor = 1.0 / math.sqrt(segments * BINS)
    rows = np.concatenate([factor * np.cos(angles), -factor * np.sin(angles)], axis=1)
    return rows.astype(np.float32).astype(ml_dtypes.bfloat16)


def band(filter_taps):
    tap_count = filter_taps.shape[0]
    margin = (tap_count - 1) // 2
    offsets = (
        jnp.arange(LANES, dtype=jnp.int32)[None, :]
        - jnp.arange(3 * LANES, dtype=jnp.int32)[:, None]
        + LANES
        + margin
    )
    match = offsets[:, :, None] == jnp.arange(tap_count, dtype=jnp.int32)[None, None, :]
    return jnp.sum(
        jnp.where(match, filter_taps.astype(jnp.float32)[None, None, :], 0.0), axis=2
    ).astype(jnp.bfloat16)


def fold_kernel(forward_ref, band_ref, fold_ref):
    for j in range(fold_ref.shape[1] // LANES):
        fold_ref[:, j * LANES : (j + 1) * LANES] = jnp.dot(
            forward_ref[:, j * LANES : (j + 3) * LANES],
            band_ref[...],
            preferred_element_type=jnp.float32,
        ).astype(fold_ref.dtype)


def folded(filter_taps):
    return pl.pallas_call(
        fold_kernel,
        out_shape=jax.ShapeDtypeStruct((NFFT, NFFT + 2 * LANES), jnp.bfloat16),
        compiler_params=pltpu.CompilerParams(vmem_limit_bytes=32 * MIB),
    )(jnp.asarray(forward_padded()), band(filter_taps))


def main_kernel(fold_ref, own_ref, refs_ref, inv_ref, valid_ref, out_ref, x, y, w, o, v, z):
    segments, own, _ = own_ref.shape
    refs = refs_ref.shape[1]
    pairs = segments // 2
    depth = 2 * segments
    dot = lambda a, b, ca, cb: lax.dot_general(
        a, b, (((ca,), (cb,)), ((), ())), preferred_element_type=jnp.float32
    )

    for g in range(segments):
        base = (g % 2) * LANES
        places = ((0, own, own_ref), (own, own, own_ref), (2 * own, refs, refs_ref))
        for start, count, source in places:
            rows = slice(base + start, base + start + count)
            edge = jnp.zeros((count, LANES), x.dtype)
            x[g // 2, rows, LANES : LANES + NFFT] = source[g]
            x[g // 2, rows, :LANES] = source[g - 1, :, NFFT - LANES :] if g else edge
            x[g // 2, rows, LANES + NFFT :] = (
                source[g + 1, :, :LANES] if g + 1 < segments else edge
            )

    chunk = 64

    def transform(p, carry):
        y[...] = dot(fold_ref[...], x[p], 1, 1)
        lane = lax.broadcasted_iota(jnp.int32, (chunk, LANES), 1)
        turned = (lane >= own) & (lane < 2 * own)
        for h in range(2):
            columns = slice(h * LANES, (h + 1) * LANES)
            total = jnp.zeros((chunk, LANES), jnp.float32)
            for c in range(BINS // chunk):
                re = y[c * chunk : (c + 1) * chunk, columns]
                im = y[BINS + c * chunk : BINS + (c + 1) * chunk, columns]
                total += re * re + im * im
            water = jnp.sum(total, axis=0, keepdims=True) * (1.0 / BINS)
            for c in range(BINS // chunk):
                re = y[c * chunk : (c + 1) * chunk, columns]
                im = y[BINS + c * chunk : BINS + (c + 1) * chunk, columns]
                factor = lax.rsqrt(re * re + im * im + water + 1e-06)
                a, b = re * factor, im * factor
                at = c * chunk * (depth + SKEW) + 2 * p + h
                w[pl.ds(at, chunk, stride=depth + SKEW), :] = jnp.where(turned, -b, a)
                w[pl.ds(at + segments, chunk, stride=depth + SKEW), :] = jnp.where(turned, a, b)
        return carry

    lax.fori_loop(0, pairs, transform, 0)

    group = LANES // depth
    both = 2 * own

    def cross(q, carry):
        parts = [
            w[pl.ds(pl.multiple_of((q * group + j) * (depth + SKEW), 8), depth), :]
            for j in range(group)
        ]
        t = jnp.concatenate(parts, axis=0)
        lane = lax.broadcasted_iota(jnp.int32, (LANES, LANES), 1)
        row = lax.broadcasted_iota(jnp.int32, (LANES, LANES), 0)
        left = t.T[:both].astype(jnp.bfloat16)
        twice = jnp.where(lane < refs, pltpu.roll(t, LANES - both, 1), t)
        right = jnp.concatenate(
            [
                jnp.where((row >= j * depth) & (row < (j + 1) * depth), twice, 0.0)
                for j in range(group)
            ],
            axis=1,
        ).astype(jnp.bfloat16)
        product = dot(left, right, 1, 0)
        for j in range(group):
            at = pl.multiple_of((q * group + j) * (both + SKEW), 8)
            o[pl.ds(at, both), :] = product[:, j * LANES : (j + 1) * LANES]
        return carry

    lax.fori_loop(0, BINS // group, cross, 0, unroll=8)

    def lags(n, carry):
        lane = lax.broadcasted_iota(jnp.int32, (BINS, LANES), 1)
        for j in range(2):
            for c in range(2):
                at = c * own + 4 * n + 2 * j
                a = o[pl.ds(at, BINS, stride=both + SKEW), :]
                b = o[pl.ds(at + 1, BINS, stride=both + SKEW), :]
                v[c * BINS : (c + 1) * BINS, j * LANES : (j + 1) * LANES] = jnp.where(
                    lane < refs, a, b
                ).astype(v.dtype)
        lagged = dot(inv_ref[...], v[...], 1, 0) * valid_ref[n]
        turned = lagged.T
        for i in range(4):
            for h in range(LAGS // LANES):
                z[h, pl.ds(4 * n + i, refs, stride=own), :] = turned[
                    i * refs : (i + 1) * refs, h * LANES : (h + 1) * LANES
                ]
        return carry

    lax.fori_loop(0, own // 4, lags, 0, unroll=2)
    for h in range(LAGS // LANES):
        out_ref[:, h * LANES : (h + 1) * LANES] = z[h]


def compute(fold, own_rows, ref_rows, pair_valid):
    segments, own, _ = own_rows.shape
    refs = ref_rows.shape[1]
    valid = pair_valid.reshape(refs, own).astype(jnp.float32).T.reshape(own // 4, 1, 4 * refs)
    f32, bf16 = jnp.float32, jnp.bfloat16
    return pl.pallas_call(
        main_kernel,
        out_shape=jax.ShapeDtypeStruct((refs * own, LAGS), f32),
        scratch_shapes=[
            pltpu.VMEM((segments // 2, 2 * LANES, NFFT + 2 * LANES), bf16),
            pltpu.VMEM((NFFT, 2 * LANES), f32),
            pltpu.VMEM((BINS * (2 * segments + SKEW), LANES), f32),
            pltpu.VMEM((BINS * (2 * own + SKEW), LANES), f32),
            pltpu.VMEM((NFFT, 2 * LANES), bf16),
            pltpu.VMEM((LAGS // LANES, refs * own, LANES), f32),
        ],
        compiler_params=pltpu.CompilerParams(vmem_limit_bytes=52 * MIB),
    )(fold, own_rows, ref_rows, jnp.asarray(inverse_rows(segments)), valid)


def by_segment(blocks):
    devices, stations, samples = blocks.shape
    if samples == NFFT:
        return blocks
    return (
        blocks.transpose(1, 0, 2)
        .reshape(stations, devices * samples // NFFT, NFFT)
        .transpose(1, 0, 2)
    )


def local(records, filter_taps, ref_owner, reference_station_order, pair_valid):
    device_count = lax.axis_size("sta")
    stations, samples = records.shape
    own = stations // device_count
    order = ref_owner[:, None] * own + reference_station_order
    ref_rows = jnp.take(records, order.reshape(-1), axis=0)
    halves = ref_rows.reshape(2, -1, samples)
    spread = jnp.tile(halves, (device_count // 2, 1, 1))
    blocks = jnp.concatenate([records.reshape(device_count, own, samples), spread], axis=1)
    blocks = lax.all_to_all(blocks, "sta", split_axis=0, concat_axis=0, tiled=True)
    own_rows, mine = blocks[:, :own], blocks[:, own:]
    other = lax.ppermute(mine, "sta", [(i, i ^ 1) for i in range(device_count)])
    first = lax.axis_index("sta") % 2 == 0
    ref_rows = jnp.concatenate(
        [jnp.where(first, mine, other), jnp.where(first, other, mine)], axis=1
    )
    out = compute(folded(filter_taps), by_segment(own_rows), by_segment(ref_rows), pair_valid)
    return out.reshape(pair_valid.shape + (LAGS,))


def solution(mesh):
    placed = (P("win", "sta"), P(), P("win"), P("win", None), P("win", None, "sta"))
    return jax.shard_map(
        local, mesh=mesh, in_specs=placed, out_specs=P("win", None, "sta", None), check_vma=False
    )
```
